256 devices in a mesh: dp: 16 (over z, core), seq: 8 (over x, y_lo), section: 2 (over y_hi).
Axes of the slice: x: 4, y: 4 (y_hi: 2, y_lo: 2; y = y_hi * 2 + y_lo), z: 8, core: 2. Of those that a mesh axis runs over, the one named last changes fastest.
Arguments:
- queries: bfloat16 [2, 16, 1024, 2048], P('section', 'dp', 'seq'), may hold values from -6 to 6
- key_values: bfloat16 [2, 16, 2, 1024, 2048], P('section', 'dp', None, 'seq'), may hold values from -18 to 18
- resid: bfloat16 [2, 16, 1024, 2048], P('section', 'dp', 'seq'), may hold values from -6 to 6
- upstream: bfloat16 [2, 16, 1024, 2048], P('section', 'dp', 'seq'), may hold values from -6 to 6
- w_out: bfloat16 [2, 2048, 2048], P('section', 'dp'), may hold values from -1 to 1
- gain: float32 [2, 2048], P('section'), may hold values from 0.25 to 1.75
- global_ids: int32 [16, 2], P('dp'), may hold values from 0 to 15, as said below
- random_ids: int32 [16, 16, 3], P('dp'), may hold values from 0 to 15, as said below
Outputs:
- grad_queries: bfloat16 [2, 16, 1024, 2048], P('section', 'dp', 'seq')
- grad_key_values: bfloat16 [2, 16, 2, 1024, 2048], P('section', 'dp', None, 'seq')
- passed: bfloat16 [2, 16, 1024, 2048], P('section', 'dp', 'seq')
- grad_w_out: float32 [2, 2048, 2048], P('section', 'dp')
The draws below stay inside these ranges and needn't reach their ends.
Inputs may be any that keep to these rules, and one draw needn't show every extreme that they name: `global_ids`: the 2 blocks of one sequence are different. `random_ids`: for each sequence, the 6 entries of the query blocks of one segment name blocks of any one segment at most 1 times.
All inputs are finite; a program needn't handle non-finite values.
Results may differ from the reference program's by a relative error of at most 0.025.
Values may be sent and summed in bfloat16 or wider, within the bound.
No kernel may reach another device: no remote copies, remote signals or barrier semaphores. Data moves between devices by JAX's collectives and lax.ppermute only.
A program may use at most 128 MiB of HBM per device.

```python
import math
import jax
import jax.numpy as jnp
from jax import lax

D = 2048
HDIM = 128
BLOCK = 64
R = 3
NG = 2
TOK_DEV = 128
HD = 2048
QB = 2
BATCH = 16
L = 1024
NBLK = 16
N_SEQ = 8
N_SECTION = 2


def draw_queries(key, part):
    key = jax.random.fold_in(key, 1)
    values = jnp.clip(1.5 * jax.random.normal(key, (N_SECTION, BATCH, L, HD), jnp.float32), -6.0, 6.0)
    return values.astype(jnp.bfloat16)


def draw_key_values(key, part):
    key = jax.random.fold_in(key, 2)
    first, second, third = jax.random.split(key, 3)
    keys = jnp.clip(jax.random.normal(first, (N_SECTION, BATCH, L, HD), jnp.float32), -6.0, 6.0)
    values = jnp.clip(jax.random.normal(second, (N_SECTION, BATCH, L, HD), jnp.float32), -6.0, 6.0)
    pairing = jax.random.permutation(third, BATCH)
    column_group = jnp.arange(HD) // (HD // BATCH)
    boosted = column_group[None, :] == pairing[:, None]
    values = values * jnp.where(boosted, 3.0, 1.0)[None, :, None, :]
    return jnp.stack([keys, values], axis=2).astype(jnp.bfloat16)


def draw_global_ids(key, part):
    key = jax.random.fold_in(key, 5)
    keys = jax.random.split(key, BATCH)

    def one_row(row_key):
        return jax.random.permutation(row_key, NBLK)[:NG]
    return jax.vmap(one_row)(keys).astype(jnp.int32)


def draw_random_ids(key, part):
    key = jax.random.fold_in(key, 7)
    segments = NBLK // QB
    slots = QB * R
    capacity = (slots + segments - 1) // segments
    pool_size = segments * capacity
    keys = jax.random.split(key, BATCH * segments)

    def one_segment(seg_key):
        first, second, third, fourth = jax.random.split(seg_key, 4)
        owners = jnp.arange(pool_size) // capacity
        heavy = jax.random.randint(first, (), 0, segments)
        ranks = jax.random.randint(second, (pool_size,), 0, 1 << 20) * pool_size + jnp.arange(pool_size)
        ranks = jnp.where(owners == heavy, jnp.arange(pool_size) - pool_size, ranks)
        order = jnp.argsort(ranks)
        picked = owners[order][:slots]
        picked = picked[jax.random.permutation(third, slots)]
        local = jax.random.randint(fourth, (slots,), 0, QB)
        return (picked * QB + local).reshape(QB, R)
    drawn = jax.vmap(one_segment)(keys)
    return drawn.reshape(BATCH, NBLK, R).astype(jnp.int32)


def block_scale(rng, shape, cuts, least, high):
    loudness, own = 1.0, jax.random.fold_in(rng, 6)
    for axis_at, parts in cuts:
        heights = jnp.exp(jax.random.uniform(jax.random.fold_in(own, axis_at), (parts,), jnp.float32, least / len(cuts), high / len(cuts)))
        loudness = loudness * jnp.repeat(heights, shape[axis_at] // parts).reshape([-1 if axis == axis_at else 1 for axis in range(len(shape))])
    return loudness


def centred(own_key, shape, spread, limit, cuts=(), kind=jnp.bfloat16):
    values = jax.random.normal(own_key, shape, jnp.float32) * spread
    if len(cuts) > 0:
        values = block_scale(own_key, shape, cuts, -0.22, 0.18) * values
    return jnp.clip(values, min=-limit, max=limit).astype(kind)


def setup_inputs(seed: int = 0) -> dict:
    seeds = jax.random.split(jax.random.key(seed), 9)
    return {
        "queries": draw_queries(jax.random.fold_in(seeds[8], 71), 0),
        "key_values": draw_key_values(jax.random.fold_in(seeds[8], 71), 0),
        "resid": centred(seeds[2], (N_SECTION, BATCH, L, D), 1.0, 6.0, ((0, 2), (1, 16), (2, 8))),
        "upstream": centred(seeds[3], (N_SECTION, BATCH, L, D), 1.0, 6.0, ((0, 2), (1, 16), (2, 8))),
        "w_out": centred(seeds[4], (N_SECTION, HD, D), (max(HD // 48, 1)) ** -0.5, 1.0, ((0, 2), (1, 16))),
        "gain": jnp.clip(1.0 + 0.15 * jax.random.normal(seeds[5], (N_SECTION, D), jnp.float32), 0.25, 1.75),
        "global_ids": draw_global_ids(jax.random.fold_in(seeds[8], 71), 0),
        "random_ids": draw_random_ids(jax.random.fold_in(seeds[8], 71), 0),
    }


def softmax_rows(scores, valid):
    masked = jnp.where(valid, scores, -1e+30)
    top = lax.optimization_barrier(jnp.max(masked, axis=-1, keepdims=True))
    raised = jnp.exp(masked - top)
    total = lax.optimization_barrier(jnp.sum(raised, axis=-1, keepdims=True))
    return raised / total

def round_low(values):
    return lax.optimization_barrier(values.astype(jnp.bfloat16)).astype(values.dtype)

def sequence_pass(query, pairs, inputs, grad_out, w_full, gain_row, glob_ids, rand_ids):
    length, width = query.shape
    heads = width // HDIM
    listed = 3 + NG + R
    scale = 1.0 / math.sqrt(HDIM)
    span = BLOCK * width
    block_pairs = pairs.reshape(2, NBLK, span)
    empty = jnp.zeros((2, 1, span), pairs.dtype)
    padded = jnp.concatenate([empty, block_pairs, empty], axis=1)
    pool = jnp.concatenate([padded, block_pairs[:, glob_ids], block_pairs[:, rand_ids.reshape(-1)]], axis=1)
    window_idx = jnp.arange(NBLK)[:, None] + jnp.arange(3)[None, :]
    glob_idx = jnp.broadcast_to(NBLK + 2 + jnp.arange(NG)[None, :], (NBLK, NG))
    rand_idx = NBLK + 2 + NG + jnp.arange(NBLK * R).reshape(NBLK, R)
    table = jnp.concatenate([window_idx, glob_idx, rand_idx], axis=1)
    gathered = jnp.take(pool, table, axis=1)
    key_list = gathered[0].reshape(NBLK, listed * BLOCK, heads, HDIM)
    value_list = gathered[1].reshape(NBLK, listed * BLOCK, heads, HDIM)
    target = window_idx - 1
    window_valid = (target >= 0) & (target < NBLK)
    valid_blocks = jnp.concatenate([window_valid, jnp.ones((NBLK, NG + R), bool)], axis=1)
    valid = jnp.repeat(valid_blocks, BLOCK, axis=1)[:, None, None, :]
    query_blocks = query.reshape(NBLK, BLOCK, heads, HDIM)
    scores = jnp.einsum('jahe,jthe->jhat', query_blocks, key_list, preferred_element_type=jnp.float32) * scale
    shares = softmax_rows(scores, valid)
    shares_low = shares.astype(jnp.bfloat16)
    attended = jnp.einsum('jhat,jthe->jahe', shares_low, value_list, preferred_element_type=jnp.float32)
    attended = attended.astype(jnp.bfloat16).reshape(length, width)
    projected = jnp.dot(attended, w_full, preferred_element_type=jnp.float32)
    summed = inputs.astype(jnp.float32) + projected
    inverse = lax.rsqrt(lax.optimization_barrier(jnp.mean(summed * summed, axis=-1, keepdims=True)) + 1e-06)
    scaled_grad = grad_out.astype(jnp.float32) * gain_row
    inner = lax.optimization_barrier(jnp.mean(scaled_grad * summed, axis=-1, keepdims=True))
    grad_sum = (inverse * scaled_grad - summed * inverse ** 3 * inner).astype(jnp.bfloat16)
    grad_attended = jnp.dot(grad_sum, w_full.T, preferred_element_type=jnp.float32).astype(jnp.bfloat16)
    seg_att = attended.reshape(N_SEQ, TOK_DEV, width)
    seg_grad = grad_sum.reshape(N_SEQ, TOK_DEV, inputs.shape[1])

    def seg_step(carry, items):
        term = jnp.einsum('th,td->hd', items[0], items[1], preferred_element_type=jnp.float32)
        return (carry + round_low(term), None)
    weight_sum, _ = lax.scan(seg_step, jnp.zeros((width, inputs.shape[1]), jnp.float32), (seg_att, seg_grad))
    grad_blocks = grad_attended.reshape(NBLK, BLOCK, heads, HDIM)
    grad_shares = jnp.einsum('jahe,jthe->jhat', grad_blocks, value_list, preferred_element_type=jnp.float32)
    centre = lax.optimization_barrier(jnp.sum(shares * grad_shares, axis=-1, keepdims=True))
    grad_scores = (shares * (grad_shares - centre) * scale).astype(jnp.bfloat16)
    grad_query = jnp.einsum('jhat,jthe->jahe', grad_scores, key_list, preferred_element_type=jnp.float32)
    grad_query = grad_query.astype(jnp.bfloat16).reshape(length, width)
    grad_keys = jnp.einsum('jhat,jahe->jthe', grad_scores, query_blocks, preferred_element_type=jnp.float32)
    grad_values = jnp.einsum('jhat,jahe->jthe', shares_low, grad_blocks, preferred_element_type=jnp.float32)
    grad_list = jnp.stack([grad_keys, grad_values]).reshape(2, NBLK, listed, span)
    window_part = grad_list[:, :, :3]
    cross = jnp.arange(NBLK)[:, None] // QB != target // QB
    window_part = jnp.where(cross[None, :, :, None], round_low(window_part), window_part)
    accum = jnp.zeros((2, NBLK + 2, span), jnp.float32).at[:, window_idx].add(window_part)
    own_grad = accum[:, 1:NBLK + 1]
    glob_part = grad_list[:, :, 3:3 + NG].reshape(2, N_SEQ, QB, NG, span)
    glob_part = lax.optimization_barrier(jnp.sum(round_low(lax.optimization_barrier(jnp.sum(glob_part, axis=2))), axis=1))
    own_grad = own_grad.at[:, glob_ids].add(glob_part)
    rand_part = round_low(grad_list[:, :, 3 + NG:]).reshape(2, NBLK * R, span)
    own_grad = own_grad.at[:, rand_ids.reshape(-1)].add(rand_part)
    grad_pairs = own_grad.astype(jnp.bfloat16).reshape(2, length, width)
    return (grad_query, grad_pairs, grad_sum, weight_sum)

def reference(queries, key_values, resid, upstream, w_out, gain, global_ids, random_ids):
    all_query, all_pairs, all_sums, all_weights = ([], [], [], [])
    for section in range(N_SECTION):

        def one_sequence(carry, items, section=section):
            grad_query, grad_pairs, grad_sum, weight_sum = sequence_pass(items[0], items[1], items[2], items[3], w_out[section], gain[section], items[4], items[5])
            return (carry + weight_sum, (grad_query, grad_pairs, grad_sum))
        start_sum = jnp.zeros((HD, D), jnp.float32)
        total, outputs = lax.scan(one_sequence, start_sum, (queries[section], key_values[section], resid[section], upstream[section], global_ids, random_ids))
        all_query.append(outputs[0])
        all_pairs.append(outputs[1])
        all_sums.append(outputs[2])
        all_weights.append(total * (1.0 / BATCH))
    grad_queries = jnp.stack(all_query)
    grad_key_values = jnp.stack(all_pairs)
    passed = jnp.stack([all_sums[(section + 1) % N_SECTION] for section in range(N_SECTION)])
    grad_w_out = jnp.stack(all_weights)
    return (grad_queries, grad_key_values, passed, grad_w_out)
```

```python
import functools
import math

import jax
import jax.numpy as jnp
from jax import lax
from jax.experimental import pallas as pl
from jax.experimental.pallas import tpu as pltpu
from jax.sharding import Mesh
from jax.sharding import PartitionSpec as P

HDIM = 128
BLOCK = 64
R = 3
NG = 2
QB = 2
N_SEQ = 8
NBLK = N_SEQ * QB
PAIR = 2 * HDIM
D = 2048
N_Z = 8
BATCH = 16
TOK = QB * BLOCK
LISTED = 3 + NG + R
SCALE = 1.0 / math.sqrt(HDIM)
NEG = -1e30
F32 = jnp.float32
BF16 = jnp.bfloat16
VMEM_LIMIT = 48 * 1024 * 1024


def dot(a, b, contract):
    return lax.dot_general(a, b, (contract, ((), ())), preferred_element_type=F32)


def diagonal(rows):
    zero = jnp.zeros((BLOCK, HDIM), rows.dtype)
    top = jnp.concatenate([rows[:, :HDIM], zero], axis=1)
    low = jnp.concatenate([zero, rows[:, HDIM:]], axis=1)
    return jnp.concatenate([top, low], axis=0)


def undiagonal(both):
    return jnp.concatenate([both[:BLOCK, :HDIM], both[BLOCK:, HDIM:]], axis=1)


def listed_blocks(j, glob_ref, rand_ref):
    window = [jnp.maximum(j - 1, 0), j, jnp.minimum(j + 1, NBLK - 1)]
    chosen = [glob_ref[g] for g in range(NG)]
    chosen += [rand_ref[j * R + r] for r in range(R)]
    return window + chosen


def take(got_ref, which, ids):
    return jnp.concatenate([got_ref[b // QB, which, b % QB] for b in ids], axis=0)


def share_columns(j, keys, query_diag):
    scores = dot(keys, query_diag, ((1,), (1,))) * SCALE
    first = jnp.where(j > 0, scores[:BLOCK], NEG)
    last = jnp.where(j < NBLK - 1, scores[2 * BLOCK : 3 * BLOCK], NEG)
    scores = jnp.concatenate(
        [first, scores[BLOCK : 2 * BLOCK], last, scores[3 * BLOCK :]], axis=0
    )
    top = jnp.max(scores, axis=0, keepdims=True)
    raised = jnp.exp(scores - top)
    total = jnp.sum(raised, axis=0, keepdims=True)
    return raised * (1.0 / total)


def forward_kernel(unroll, glob_ref, rand_ref, got_ref, att_ref):
    def one(j):
        ids = listed_blocks(j, glob_ref, rand_ref)
        keys = take(got_ref, 1, ids)
        values = take(got_ref, 2, ids)
        query_diag = diagonal(got_ref[j // QB, 0, j % QB])
        shares = share_columns(j, keys, query_diag).astype(BF16)
        att = dot(shares, values, ((0,), (0,)))
        att_ref[j // QB, j % QB] = undiagonal(att).astype(BF16)

    def step(g, carry):
        for u in range(unroll):
            one(g * unroll + u)
        return carry

    lax.fori_loop(0, NBLK // unroll, step, 0)


def backward_kernel(unroll, glob_ref, rand_ref, got_ref, grad_ref, out_ref, acc, glob_acc, rand_acc):
    acc[...] = jnp.zeros_like(acc)
    glob_acc[...] = jnp.zeros_like(glob_acc)
    rand_acc[...] = jnp.zeros_like(rand_acc)

    def one(j):
        ids = listed_blocks(j, glob_ref, rand_ref)
        keys = take(got_ref, 1, ids)
        values = take(got_ref, 2, ids)
        query_diag = diagonal(got_ref[j // QB, 0, j % QB])
        grad_diag = diagonal(grad_ref[j // QB, j % QB])
        shares = share_columns(j, keys, query_diag)
        grad_shares = dot(values, grad_diag, ((1,), (1,)))
        centre = jnp.sum(shares * grad_shares, axis=0, keepdims=True)
        grad_scores = (shares * (grad_shares - centre) * SCALE).astype(BF16)
        grad_query = dot(grad_scores, keys, ((0,), (0,)))
        out_ref[j // QB, 0, j % QB] = undiagonal(grad_query).astype(BF16)
        parts = (
            dot(grad_scores, query_diag, ((1,), (0,))),
            dot(shares.astype(BF16), grad_diag, ((1,), (0,))),
        )
        for which in range(2):
            part = parts[which]
            for n in range(3):
                acc[which, ids[n]] += part[n * BLOCK : (n + 1) * BLOCK]
            glob_acc[which] += part[3 * BLOCK : (3 + NG) * BLOCK]
            for n in range(3 + NG, LISTED):
                rand_acc[which, ids[n]] += part[n * BLOCK : (n + 1) * BLOCK]

    def step(g, carry):
        for u in range(unroll):
            one(g * unroll + u)
        return carry

    lax.fori_loop(0, NBLK // unroll, step, 0)
    for which in range(2):
        for g in range(NG):
            acc[which, glob_ref[g]] += glob_acc[which, g * BLOCK : (g + 1) * BLOCK]

    def finish(b, carry):
        for which in range(2):
            total = acc[which, b] + rand_acc[which, b]
            out_ref[b // QB, 1 + which, b % QB] = total.astype(BF16)
        return carry

    lax.fori_loop(0, NBLK, finish, 0)


def project_kernel(att_ref, w_hbm, resid_ref, up_ref, gain_ref, sum_ref, ga_ref, w_vmem, total, sems):
    copies = [
        pltpu.make_async_copy(
            w_hbm.at[pl.ds(s * PAIR, PAIR)], w_vmem.at[pl.ds(s * PAIR, PAIR)], sems.at[s]
        )
        for s in range(N_SEQ)
    ]
    for copy in copies:
        copy.start()
    total[...] = resid_ref[...].astype(F32)
    for s in range(N_SEQ):
        copies[s].wait()
        total[...] += dot(att_ref[s], w_vmem[s * PAIR : (s + 1) * PAIR], ((1,), (0,)))
    summed = total[...]
    inverse = lax.rsqrt(jnp.mean(summed * summed, axis=-1, keepdims=True) + 1e-06)
    scaled = up_ref[...].astype(F32) * gain_ref[...]
    inner = jnp.mean(scaled * summed, axis=-1, keepdims=True)
    grad_sum = (inverse * scaled - summed * (inverse * inverse * inverse * inner)).astype(BF16)
    sum_ref[...] = grad_sum
    for s in range(N_SEQ):
        part = dot(grad_sum, w_vmem[s * PAIR : (s + 1) * PAIR], ((1,), (1,)))
        ga_ref[s] = part.astype(BF16)


def term_kernel(own_ref, other_ref, own_sum_ref, other_sum_ref, out_ref):
    for n in range(N_Z):
        part = dot(own_ref[n], own_sum_ref[...], ((0,), (0,)))
        part += dot(other_ref[n], other_sum_ref[...], ((0,), (0,)))
        out_ref[n] = part.astype(BF16)


def split_kernel(rows_ref, after_ref, out_ref):
    for s in range(N_SEQ):
        out_ref[s] = rows_ref[:, s * PAIR : (s + 1) * PAIR]


def spread_kernel(parts_ref, out_ref):
    total = parts_ref[0].astype(F32)
    for n in range(1, N_SEQ):
        total += parts_ref[n].astype(F32)
    total = total.astype(BF16)
    for s in range(N_SEQ):
        out_ref[s] = total


def average_kernel(pieces_ref, out_ref):
    for s in range(N_SEQ):
        out_ref[:, s * PAIR : (s + 1) * PAIR] = pieces_ref[s].astype(F32) * (1.0 / BATCH)


def vmem():
    return pl.BlockSpec(memory_space=pltpu.VMEM)


def anywhere():
    return pl.BlockSpec(memory_space=pl.ANY)


def smem():
    return pl.BlockSpec(memory_space=pltpu.SMEM)


def call(kernel, name, out_shape, in_specs, out_specs, scratch=(), flops=0, moved=0):
    return pl.pallas_call(
        kernel,
        out_shape=out_shape,
        in_specs=in_specs,
        out_specs=out_specs,
        scratch_shapes=list(scratch),
        compiler_params=pltpu.CompilerParams(vmem_limit_bytes=VMEM_LIMIT),
        cost_estimate=pl.CostEstimate(flops=flops, bytes_accessed=moved, transcendentals=0),
        name=name,
    )


def exchange(chunks):
    return lax.all_to_all(chunks, "seq", 0, 0, tiled=True)


def on_device(queries, key_values, resid, upstream, w_out, gain, global_ids, random_ids):
    core = lax.axis_index("core")
    swap = [(0, 1), (1, 0)]
    glob_ids = global_ids[0]
    rand_ids = random_ids[0].reshape(NBLK * R)

    with jax.named_scope("gather_w"):
        w_full = lax.all_gather(w_out[0], ("z", "core"), axis=0, tiled=True)

    with jax.named_scope("to_heads"):
        packed = jnp.concatenate([queries[0], key_values[0, 0]], axis=0)
        packed = packed.reshape(3, TOK, N_SEQ, PAIR).transpose(2, 0, 1, 3)
        got = exchange(packed).reshape(N_SEQ, 3, QB, BLOCK, PAIR)

    with jax.named_scope("forward"):
        att = call(
            functools.partial(forward_kernel, 8),
            "attention_forward",
            jax.ShapeDtypeStruct((N_SEQ, QB, BLOCK, PAIR), BF16),
            [smem(), smem(), vmem()],
            vmem(),
            flops=1_000_000_000,
            moved=2_000_000,
        )(glob_ids, rand_ids, got)

    with jax.named_scope("to_tokens"):
        att = exchange(att.reshape(N_SEQ, TOK, PAIR))

    with jax.named_scope("project"):
        grad_sum, grad_att = call(
            project_kernel,
            "project",
            (
                jax.ShapeDtypeStruct((TOK, D), BF16),
                jax.ShapeDtypeStruct((N_SEQ, TOK, PAIR), BF16),
            ),
            [vmem(), anywhere(), vmem(), vmem(), vmem()],
            (vmem(), vmem()),
            [
                pltpu.VMEM((D, D), BF16),
                pltpu.VMEM((TOK, D), F32),
                pltpu.SemaphoreType.DMA((N_SEQ,)),
            ],
            flops=2_000_000_000,
            moved=10_000_000,
        )(att, w_full, resid[0, 0], upstream[0, 0], gain)

    with jax.named_scope("grad_to_heads"):
        grad_got = exchange(grad_att).reshape(N_SEQ, QB, BLOCK, PAIR)

    with jax.named_scope("weight_grad"):
        halves = att.reshape(N_SEQ, TOK, 2, HDIM)
        own = jnp.where(core == 0, halves[:, :, 0], halves[:, :, 1])
        given = jnp.where(core == 0, halves[:, :, 1], halves[:, :, 0])
        other = lax.ppermute(given, "core", swap)
        other_sum = lax.ppermute(grad_sum, "core", swap)
        term = call(
            term_kernel,
            "weight_term",
            jax.ShapeDtypeStruct((N_Z, HDIM, D), BF16),
            [vmem()] * 4,
            vmem(),
            flops=1_000_000_000,
            moved=6_000_000,
        )(own, other, grad_sum, other_sum)
        shard = lax.psum_scatter(
            term.reshape(N_Z * HDIM, D), "z", scatter_dimension=0, tiled=True
        )

    with jax.named_scope("passed"):
        passed = lax.ppermute(grad_sum, "section", swap)

    with jax.named_scope("backward"):
        grads = call(
            functools.partial(backward_kernel, 8),
            "attention_backward",
            jax.ShapeDtypeStruct((N_SEQ, 3, QB, BLOCK, PAIR), BF16),
            [smem(), smem(), vmem(), vmem()],
            vmem(),
            [
                pltpu.VMEM((2, NBLK, BLOCK, PAIR), F32),
                pltpu.VMEM((2, NG * BLOCK, PAIR), F32),
                pltpu.VMEM((2, NBLK, BLOCK, PAIR), F32),
            ],
            flops=3_000_000_000,
            moved=4_000_000,
        )(glob_ids, rand_ids, got, grad_got)

    with jax.named_scope("grads_to_tokens"):
        back = exchange(grads.reshape(N_SEQ, 3, TOK, PAIR))

    with jax.named_scope("weight_grad"):
        pieces = call(
            split_kernel,
            "weight_split",
            jax.ShapeDtypeStruct((N_SEQ, HDIM, PAIR), BF16),
            [vmem(), anywhere()],
            vmem(),
            flops=1_000_000,
            moved=1_000_000,
        )(shard, back)
        spread = call(
            spread_kernel,
            "weight_sum",
            jax.ShapeDtypeStruct((N_SEQ, HDIM, PAIR), BF16),
            [vmem()],
            vmem(),
            flops=1_000_000,
            moved=1_000_000,
        )(exchange(pieces))
        weight_grad = call(
            average_kernel,
            "average",
            jax.ShapeDtypeStruct((HDIM, D), F32),
            [vmem()],
            vmem(),
            flops=1_000_000,
            moved=1_500_000,
        )(exchange(spread))

    with jax.named_scope("unpack"):
        back = back.transpose(1, 2, 0, 3).reshape(3, TOK, D)
    return (back[None, :1].reshape(1, 1, TOK, D), back[None, None, 1:], passed[None, None], weight_grad[None])


def solution(mesh):
    fine = Mesh(mesh.devices.reshape(8, 2, 8, 2), ("z", "core", "seq", "section"))
    dp = ("z", "core")
    tokens = P("section", dp, "seq", None)
    pairs = P("section", dp, None, "seq", None)
    rows = P("section", dp, None)
    return jax.shard_map(
        on_device,
        mesh=fine,
        in_specs=(
            tokens,
            pairs,
            tokens,
            tokens,
            rows,
            P("section", None),
            P(dp, None),
            P(dp, None, None),
        ),
        out_specs=(tokens, pairs, tokens, rows),
        check_vma=False,
    )
```

```python
import functools
import math

import jax
import jax.numpy as jnp
from jax import lax
from jax.experimental import pallas as pl
from jax.experimental.pallas import tpu as pltpu
from jax.sharding import Mesh
from jax.sharding import PartitionSpec as P

HDIM = 128
BLOCK = 64
R = 3
NG = 2
QB = 2
N_SEQ = 8
NBLK = N_SEQ * QB
PAIR = 2 * HDIM
D = 2048
N_Z = 8
BATCH = 16
TOK = QB * BLOCK
LISTED = 3 + NG + R
SCALE = 1.0 / math.sqrt(HDIM)
NEG = -1e30
F32 = jnp.float32
BF16 = jnp.bfloat16
VMEM_LIMIT = 48 * 1024 * 1024


def dot(a, b, contract):
    return lax.dot_general(a, b, (contract, ((), ())), preferred_element_type=F32)


def diagonal(rows):
    zero = jnp.zeros((BLOCK, HDIM), rows.dtype)
    top = jnp.concatenate([rows[:, :HDIM], zero], axis=1)
    low = jnp.concatenate([zero, rows[:, HDIM:]], axis=1)
    return jnp.concatenate([top, low], axis=0)


def undiagonal(both):
    return jnp.concatenate([both[:BLOCK, :HDIM], both[BLOCK:, HDIM:]], axis=1)


def listed_blocks(j, glob_ref, rand_ref):
    window = [jnp.maximum(j - 1, 0), j, jnp.minimum(j + 1, NBLK - 1)]
    chosen = [glob_ref[g] for g in range(NG)]
    chosen += [rand_ref[j * R + r] for r in range(R)]
    return window + chosen


def take(got_ref, which, ids):
    return jnp.concatenate([got_ref[b // QB, which, b % QB] for b in ids], axis=0)


def share_columns(j, keys, query_diag):
    scores = dot(keys, query_diag, ((1,), (1,))) * SCALE
    first = jnp.where(j > 0, scores[:BLOCK], NEG)
    last = jnp.where(j < NBLK - 1, scores[2 * BLOCK : 3 * BLOCK], NEG)
    scores = jnp.concatenate(
        [first, scores[BLOCK : 2 * BLOCK], last, scores[3 * BLOCK :]], axis=0
    )
    top = jnp.max(scores, axis=0, keepdims=True)
    raised = jnp.exp(scores - top)
    total = jnp.sum(raised, axis=0, keepdims=True)
    return raised * (1.0 / total)


def forward_kernel(unroll, glob_ref, rand_ref, got_ref, att_ref):
    def one(j):
        ids = listed_blocks(j, glob_ref, rand_ref)
        keys = take(got_ref, 1, ids)
        values = take(got_ref, 2, ids)
        query_diag = diagonal(got_ref[j // QB, 0, j % QB])
        shares = share_columns(j, keys, query_diag).astype(BF16)
        att = dot(shares, values, ((0,), (0,)))
        att_ref[j // QB, j % QB] = undiagonal(att).astype(BF16)

    def step(g, carry):
        for u in range(unroll):
            one(g * unroll + u)
        return carry

    lax.fori_loop(0, NBLK // unroll, step, 0)


def backward_kernel(unroll, glob_ref, rand_ref, got_ref, grad_ref, out_ref, acc, glob_acc, rand_acc):
    acc[...] = jnp.zeros_like(acc)
    glob_acc[...] = jnp.zeros_like(glob_acc)
    rand_acc[...] = jnp.zeros_like(rand_acc)

    def one(j):
        ids = listed_blocks(j, glob_ref, rand_ref)
        keys = take(got_ref, 1, ids)
        values = take(got_ref, 2, ids)
        query_diag = diagonal(got_ref[j // QB, 0, j % QB])
        grad_diag = diagonal(grad_ref[j // QB, j % QB])
        shares = share_columns(j, keys, query_diag)
        grad_shares = dot(values, grad_diag, ((1,), (1,)))
        centre = jnp.sum(shares * grad_shares, axis=0, keepdims=True)
        grad_scores = (shares * (grad_shares - centre) * SCALE).astype(BF16)
        grad_query = dot(grad_scores, keys, ((0,), (0,)))
        out_ref[j // QB, 0, j % QB] = undiagonal(grad_query).astype(BF16)
        parts = (
            dot(grad_scores, query_diag, ((1,), (0,))),
            dot(shares.astype(BF16), grad_diag, ((1,), (0,))),
        )
        for which in range(2):
            part = parts[which]
            for n in range(3):
                acc[which, ids[n]] += part[n * BLOCK : (n + 1) * BLOCK]
            glob_acc[which] += part[3 * BLOCK : (3 + NG) * BLOCK]
            for n in range(3 + NG, LISTED):
                rand_acc[which, ids[n]] += part[n * BLOCK : (n + 1) * BLOCK]

    def step(g, carry):
        for u in range(unroll):
            one(g * unroll + u)
        return carry

    lax.fori_loop(0, NBLK // unroll, step, 0)
    for which in range(2):
        for g in range(NG):
            acc[which, glob_ref[g]] += glob_acc[which, g * BLOCK : (g + 1) * BLOCK]

    def finish(b, carry):
        for which in range(2):
            total = acc[which, b] + rand_acc[which, b]
            out_ref[b // QB, 1 + which, b % QB] = total.astype(BF16)
        return carry

    lax.fori_loop(0, NBLK, finish, 0)


def project_kernel(att_ref, w_hbm, resid_ref, up_ref, gain_ref, sum_ref, ga_ref, w_vmem, total, sems):
    copies = [
        pltpu.make_async_copy(
            w_hbm.at[pl.ds(s * PAIR, PAIR)], w_vmem.at[pl.ds(s * PAIR, PAIR)], sems.at[s]
        )
        for s in range(N_SEQ)
    ]
    for copy in copies:
        copy.start()
    total[...] = resid_ref[...].astype(F32)
    for s in range(N_SEQ):
        copies[s].wait()
        total[...] += dot(att_ref[s], w_vmem[s * PAIR : (s + 1) * PAIR], ((1,), (0,)))
    summed = total[...]
    inverse = lax.rsqrt(jnp.mean(summed * summed, axis=-1, keepdims=True) + 1e-06)
    scaled = up_ref[...].astype(F32) * gain_ref[...]
    inner = jnp.mean(scaled * summed, axis=-1, keepdims=True)
    grad_sum = (inverse * scaled - summed * (inverse * inverse * inverse * inner)).astype(BF16)
    sum_ref[...] = grad_sum
    for s in range(N_SEQ):
        part = dot(grad_sum, w_vmem[s * PAIR : (s + 1) * PAIR], ((1,), (1,)))
        ga_ref[s] = part.astype(BF16)


def term_kernel(core_ref, own_ref, other_ref, own_sum_ref, other_sum_ref, out_hbm, held, sems):
    columns = pl.ds(pl.multiple_of(core_ref[0] * HDIM, HDIM), HDIM)
    copies = []
    for n in range(N_Z):
        part = dot(own_ref[n, :, columns], own_sum_ref[...], ((0,), (0,)))
        part += dot(other_ref[n, :, columns], other_sum_ref[...], ((0,), (0,)))
        part = part.astype(BF16)
        for s in range(N_SEQ):
            held[n, s] = part[:, s * PAIR : (s + 1) * PAIR]
        copies.append(pltpu.make_async_copy(held.at[n], out_hbm.at[n], sems.at[n]))
        copies[-1].start()
    for copy in copies:
        copy.wait()


def touch_kernel(rows_hbm, after_hbm, out_hbm, sem):
    copy = pltpu.make_async_copy(rows_hbm, out_hbm, sem)
    copy.start()
    copy.wait()


def unpack_kernel(back_hbm, query_hbm, pairs_hbm, sems):
    copies = []
    for s in range(N_SEQ):
        at = pl.ds(s * PAIR, PAIR)
        copies += [
            pltpu.make_async_copy(back_hbm.at[s, 0], query_hbm.at[:, at], sems.at[s, 0]),
            pltpu.make_async_copy(
                back_hbm.at[s, pl.ds(1, 2)], pairs_hbm.at[:, :, at], sems.at[s, 1]
            ),
        ]
    for copy in copies:
        copy.start()
    for copy in copies:
        copy.wait()


def spread_kernel(parts_ref, out_ref):
    total = parts_ref[0].astype(F32)
    for n in range(1, N_SEQ):
        total += parts_ref[n].astype(F32)
    total = total.astype(BF16)
    for s in range(N_SEQ):
        out_ref[s] = total


def average_kernel(pieces_ref, out_ref):
    for s in range(N_SEQ):
        out_ref[:, s * PAIR : (s + 1) * PAIR] = pieces_ref[s].astype(F32) * (1.0 / BATCH)


def vmem():
    return pl.BlockSpec(memory_space=pltpu.VMEM)


def anywhere():
    return pl.BlockSpec(memory_space=pl.ANY)


def smem():
    return pl.BlockSpec(memory_space=pltpu.SMEM)


def call(kernel, name, out_shape, in_specs, out_specs, scratch=(), flops=0, moved=0):
    return pl.pallas_call(
        kernel,
        out_shape=out_shape,
        in_specs=in_specs,
        out_specs=out_specs,
        scratch_shapes=list(scratch),
        compiler_params=pltpu.CompilerParams(vmem_limit_bytes=VMEM_LIMIT),
        cost_estimate=pl.CostEstimate(flops=flops, bytes_accessed=moved, transcendentals=0),
        name=name,
    )


def exchange(chunks):
    return lax.all_to_all(chunks, "seq", 0, 0, tiled=True)


def on_device(queries, key_values, resid, upstream, w_out, gain, global_ids, random_ids):
    core = lax.axis_index("core")
    swap = [(0, 1), (1, 0)]
    glob_ids = global_ids[0]
    rand_ids = random_ids[0].reshape(NBLK * R)

    with jax.named_scope("gather_w"):
        w_full = lax.all_gather(w_out[0], ("z", "core"), axis=0, tiled=True)

    with jax.named_scope("to_heads"):
        packed = jnp.concatenate([queries[0], key_values[0, 0]], axis=0)
        packed = packed.reshape(3, TOK, N_SEQ, PAIR).transpose(2, 0, 1, 3)
        got = exchange(packed).reshape(N_SEQ, 3, QB, BLOCK, PAIR)

    with jax.named_scope("forward"):
        att = call(
            functools.partial(forward_kernel, 8),
            "attention_forward",
            jax.ShapeDtypeStruct((N_SEQ, QB, BLOCK, PAIR), BF16),
            [smem(), smem(), vmem()],
            vmem(),
            flops=1_000_000_000,
            moved=2_000_000,
        )(glob_ids, rand_ids, got)

    with jax.named_scope("to_tokens"):
        att = exchange(att.reshape(N_SEQ, TOK, PAIR))

    with jax.named_scope("project"):
        grad_sum, grad_att = call(
            project_kernel,
            "project",
            (
                jax.ShapeDtypeStruct((TOK, D), BF16),
                jax.ShapeDtypeStruct((N_SEQ, TOK, PAIR), BF16),
            ),
            [vmem(), anywhere(), vmem(), vmem(), vmem()],
            (vmem(), vmem()),
            [
                pltpu.VMEM((D, D), BF16),
                pltpu.VMEM((TOK, D), F32),
                pltpu.SemaphoreType.DMA((N_SEQ,)),
            ],
            flops=2_000_000_000,
            moved=10_000_000,
        )(att, w_full, resid[0, 0], upstream[0, 0], gain)

    with jax.named_scope("grad_to_heads"):
        grad_got = exchange(grad_att).reshape(N_SEQ, QB, BLOCK, PAIR)

    with jax.named_scope("weight_grad"):
        other = lax.ppermute(att, "core", swap)
        other_sum = lax.ppermute(grad_sum, "core", swap)
        term = call(
            term_kernel,
            "weight_term",
            jax.ShapeDtypeStruct((N_Z, N_SEQ, HDIM, PAIR), BF16),
            [smem()] + [vmem()] * 4,
            anywhere(),
            [
                pltpu.VMEM((N_Z, N_SEQ, HDIM, PAIR), BF16),
                pltpu.SemaphoreType.DMA((N_Z,)),
            ],
            flops=1_000_000_000,
            moved=6_000_000,
        )(core.reshape(1).astype(jnp.int32), att, other, grad_sum, other_sum)
        shard = lax.psum_scatter(term, "z", scatter_dimension=0, tiled=True)[0]

    with jax.named_scope("passed"):
        later = call(
            touch_kernel,
            "later",
            jax.ShapeDtypeStruct((TOK, D), BF16),
            [anywhere(), anywhere()],
            anywhere(),
            [pltpu.SemaphoreType.DMA(())],
            flops=1_000_000,
            moved=1_000_000,
        )(grad_sum, grad_got)
        passed = lax.ppermute(later, "section", swap)

    with jax.named_scope("backward"):
        grads = call(
            functools.partial(backward_kernel, 8),
            "attention_backward",
            jax.ShapeDtypeStruct((N_SEQ, 3, QB, BLOCK, PAIR), BF16),
            [smem(), smem(), vmem(), vmem()],
            vmem(),
            [
                pltpu.VMEM((2, NBLK, BLOCK, PAIR), F32),
                pltpu.VMEM((2, NG * BLOCK, PAIR), F32),
                pltpu.VMEM((2, NBLK, BLOCK, PAIR), F32),
            ],
            flops=3_000_000_000,
            moved=4_000_000,
        )(glob_ids, rand_ids, got, grad_got)

    with jax.named_scope("grads_to_tokens"):
        back = exchange(grads.reshape(N_SEQ, 3, TOK, PAIR))

    with jax.named_scope("unpack"):
        grad_query, grad_pairs = call(
            unpack_kernel,
            "unpack",
            (
                jax.ShapeDtypeStruct((TOK, D), BF16),
                jax.ShapeDtypeStruct((2, TOK, D), BF16),
            ),
            [anywhere()],
            (anywhere(), anywhere()),
            [pltpu.SemaphoreType.DMA((N_SEQ, 2))],
            flops=1_000_000,
            moved=3_000_000,
        )(back)

    with jax.named_scope("weight_grad"):
        shard, grad_query = lax.optimization_barrier((shard, grad_query))
        spread = call(
            spread_kernel,
            "weight_sum",
            jax.ShapeDtypeStruct((N_SEQ, HDIM, PAIR), BF16),
            [vmem()],
            vmem(),
            flops=1_000_000,
            moved=1_000_000,
        )(exchange(shard))
        spread, passed = lax.optimization_barrier((spread, passed))
        weight_grad = call(
            average_kernel,
            "average",
            jax.ShapeDtypeStruct((HDIM, D), F32),
            [vmem()],
            vmem(),
            flops=1_000_000,
            moved=1_500_000,
        )(exchange(spread))

    return (
        grad_query[None, None],
        grad_pairs[None, None],
        passed[None, None],
        weight_grad[None],
    )


def solution(mesh):
    fine = Mesh(mesh.devices.reshape(8, 2, 8, 2), ("z", "core", "seq", "section"))
    dp = ("z", "core")
    tokens = P("section", dp, "seq", None)
    pairs = P("section", dp, None, "seq", None)
    rows = P("section", dp, None)
    return jax.shard_map(
        on_device,
        mesh=fine,
        in_specs=(
            tokens,
            pairs,
            tokens,
            tokens,
            rows,
            P("section", None),
            P(dp, None),
            P(dp, None, None),
        ),
        out_specs=(tokens, pairs, tokens, rows),
        check_vma=False,
    )
```

```python
import functools
import math

import jax
import jax.numpy as jnp
from jax import lax
from jax.experimental import pallas as pl
from jax.experimental.pallas import tpu as pltpu
from jax.sharding import Mesh
from jax.sharding import PartitionSpec as P

HDIM = 128
BLOCK = 64
R = 3
NG = 2
QB = 2
N_SEQ = 8
NBLK = N_SEQ * QB
PAIR = 2 * HDIM
D = 2048
STAGE = 2
N_Z = 8
BATCH = 16
TOK = QB * BLOCK
LISTED = 3 + NG + R
SCALE = 1.0 / math.sqrt(HDIM)
NEG = -1e30
F32 = jnp.float32
BF16 = jnp.bfloat16
VMEM_LIMIT = 48 * 1024 * 1024


def dot(a, b, contract):
    return lax.dot_general(a, b, (contract, ((), ())), preferred_element_type=F32)


def diagonal(rows):
    zero = jnp.zeros((BLOCK, HDIM), rows.dtype)
    top = jnp.concatenate([rows[:, :HDIM], zero], axis=1)
    low = jnp.concatenate([zero, rows[:, HDIM:]], axis=1)
    return jnp.concatenate([top, low], axis=0)


def undiagonal(both):
    return jnp.concatenate([both[:BLOCK, :HDIM], both[BLOCK:, HDIM:]], axis=1)


def listed_blocks(j, glob_ref, rand_ref):
    window = [jnp.maximum(j - 1, 0), j, jnp.minimum(j + 1, NBLK - 1)]
    chosen = [glob_ref[g] for g in range(NG)]
    chosen += [rand_ref[j * R + r] for r in range(R)]
    return window + chosen


def take(got_ref, which, ids):
    return jnp.concatenate([got_ref[b // QB, which, b % QB] for b in ids], axis=0)


def share_columns(j, keys, query_diag):
    scores = dot(keys, query_diag, ((1,), (1,))) * SCALE
    first = jnp.where(j > 0, scores[:BLOCK], NEG)
    last = jnp.where(j < NBLK - 1, scores[2 * BLOCK : 3 * BLOCK], NEG)
    scores = jnp.concatenate(
        [first, scores[BLOCK : 2 * BLOCK], last, scores[3 * BLOCK :]], axis=0
    )
    top = jnp.max(scores, axis=0, keepdims=True)
    raised = jnp.exp(scores - top)
    total = jnp.sum(raised, axis=0, keepdims=True)
    return raised * (1.0 / total)


def forward_kernel(unroll, glob_ref, rand_ref, got_ref, att_ref):
    def one(j):
        ids = listed_blocks(j, glob_ref, rand_ref)
        keys = take(got_ref, 1, ids)
        values = take(got_ref, 2, ids)
        query_diag = diagonal(got_ref[j // QB, 0, j % QB])
        shares = share_columns(j, keys, query_diag).astype(BF16)
        att = dot(shares, values, ((0,), (0,)))
        att_ref[j // QB, j % QB] = undiagonal(att).astype(BF16)

    def step(g, carry):
        for u in range(unroll):
            one(g * unroll + u)
        return carry

    lax.fori_loop(0, NBLK // unroll, step, 0)


def backward_kernel(unroll, glob_ref, rand_ref, got_ref, grad_ref, out_ref, acc, glob_acc, rand_acc):
    acc[...] = jnp.zeros_like(acc)
    glob_acc[...] = jnp.zeros_like(glob_acc)
    rand_acc[...] = jnp.zeros_like(rand_acc)

    def one(j):
        ids = listed_blocks(j, glob_ref, rand_ref)
        keys = take(got_ref, 1, ids)
        values = take(got_ref, 2, ids)
        query_diag = diagonal(got_ref[j // QB, 0, j % QB])
        grad_diag = diagonal(grad_ref[j // QB, j % QB])
        shares = share_columns(j, keys, query_diag)
        grad_shares = dot(values, grad_diag, ((1,), (1,)))
        centre = jnp.sum(shares * grad_shares, axis=0, keepdims=True)
        grad_scores = (shares * (grad_shares - centre) * SCALE).astype(BF16)
        grad_query = dot(grad_scores, keys, ((0,), (0,)))
        out_ref[j // QB, 0, j % QB] = undiagonal(grad_query).astype(BF16)
        parts = (
            dot(grad_scores, query_diag, ((1,), (0,))),
            dot(shares.astype(BF16), grad_diag, ((1,), (0,))),
        )
        for which in range(2):
            part = parts[which]
            for n in range(3):
                acc[which, ids[n]] += part[n * BLOCK : (n + 1) * BLOCK]
            glob_acc[which] += part[3 * BLOCK : (3 + NG) * BLOCK]
            for n in range(3 + NG, LISTED):
                rand_acc[which, ids[n]] += part[n * BLOCK : (n + 1) * BLOCK]

    def step(g, carry):
        for u in range(unroll):
            one(g * unroll + u)
        return carry

    lax.fori_loop(0, NBLK // unroll, step, 0)
    for which in range(2):
        for g in range(NG):
            acc[which, glob_ref[g]] += glob_acc[which, g * BLOCK : (g + 1) * BLOCK]

    def finish(b, carry):
        for which in range(2):
            total = acc[which, b] + rand_acc[which, b]
            out_ref[b // QB, 1 + which, b % QB] = total.astype(BF16)
        return carry

    lax.fori_loop(0, NBLK, finish, 0)


def project_kernel(
    att_ref, w_hbm, resid_ref, up_ref, gain_ref, sum_hbm, ga_ref, w_vmem, total, held, sems, sum_sem
):
    copies = [
        pltpu.make_async_copy(
            w_hbm.at[pl.ds(s * PAIR, PAIR)], w_vmem.at[pl.ds(s * PAIR, PAIR)], sems.at[s]
        )
        for s in range(N_SEQ)
    ]
    for copy in copies:
        copy.start()
    for s in range(0, N_SEQ, STAGE):
        for n in range(s, s + STAGE):
            copies[n].wait()
        att = jnp.concatenate([att_ref[n] for n in range(s, s + STAGE)], axis=1)
        part = dot(att, w_vmem[s * PAIR : (s + STAGE) * PAIR], ((1,), (0,)))
        total[...] = part + (resid_ref[...].astype(F32) if s == 0 else total[...])
    summed = total[...]
    inverse = lax.rsqrt(jnp.mean(summed * summed, axis=-1, keepdims=True) + 1e-06)
    scaled = up_ref[...].astype(F32) * gain_ref[...]
    inner = jnp.mean(scaled * summed, axis=-1, keepdims=True)
    grad_sum = (inverse * scaled - summed * (inverse * inverse * inverse * inner)).astype(BF16)
    held[...] = grad_sum
    out = pltpu.make_async_copy(held, sum_hbm, sum_sem)
    out.start()
    for s in range(N_SEQ):
        part = dot(grad_sum, w_vmem[s * PAIR : (s + 1) * PAIR], ((1,), (1,)))
        ga_ref[s] = part.astype(BF16)
    out.wait()


def term_kernel(core_ref, own_ref, other_ref, own_sum_ref, other_sum_ref, out_hbm, held, sums, sems):
    columns = pl.ds(pl.multiple_of(core_ref[0] * HDIM, HDIM), HDIM)
    sums[:TOK] = own_sum_ref[...]
    sums[TOK:] = other_sum_ref[...]
    copies = []
    for n in range(N_Z):
        both = jnp.concatenate([own_ref[n, :, columns], other_ref[n, :, columns]], axis=0)
        part = dot(both, sums[...], ((0,), (0,))).astype(BF16)
        for s in range(N_SEQ):
            held[n, s] = part[:, s * PAIR : (s + 1) * PAIR]
        copies.append(pltpu.make_async_copy(held.at[n], out_hbm.at[n], sems.at[n]))
        copies[-1].start()
    for copy in copies:
        copy.wait()


def touch_kernel(rows_hbm, *refs):
    out_hbm, sem = refs[-2:]
    copy = pltpu.make_async_copy(rows_hbm, out_hbm, sem)
    copy.start()
    copy.wait()


def unpack_kernel(back_hbm, query_hbm, pairs_hbm, sems):
    copies = []
    for s in range(N_SEQ):
        at = pl.ds(s * PAIR, PAIR)
        copies += [
            pltpu.make_async_copy(back_hbm.at[s, 0], query_hbm.at[:, at], sems.at[s, 0]),
            pltpu.make_async_copy(
                back_hbm.at[s, pl.ds(1, 2)], pairs_hbm.at[:, :, at], sems.at[s, 1]
            ),
        ]
    for copy in copies:
        copy.start()
    for copy in copies:
        copy.wait()


def spread_kernel(parts_ref, out_ref):
    total = parts_ref[0].astype(F32)
    for n in range(1, N_SEQ):
        total += parts_ref[n].astype(F32)
    total = total.astype(BF16)
    for s in range(N_SEQ):
        out_ref[s] = total


def average_kernel(pieces_ref, out_hbm, held, sems):
    copies = []
    for s in range(N_SEQ):
        at = pl.ds(s * PAIR, PAIR)
        held[:, at] = pieces_ref[s].astype(F32) * (1.0 / BATCH)
        copies.append(pltpu.make_async_copy(held.at[:, at], out_hbm.at[:, at], sems.at[s]))
        copies[-1].start()
    for copy in copies:
        copy.wait()


def vmem():
    return pl.BlockSpec(memory_space=pltpu.VMEM)


def hbm():
    return pl.BlockSpec(memory_space=pltpu.HBM)


def anywhere():
    return pl.BlockSpec(memory_space=pl.ANY)


def smem():
    return pl.BlockSpec(memory_space=pltpu.SMEM)


def call(kernel, name, out_shape, in_specs, out_specs, scratch=(), flops=0, moved=0):
    return pl.pallas_call(
        kernel,
        out_shape=out_shape,
        in_specs=in_specs,
        out_specs=out_specs,
        scratch_shapes=list(scratch),
        compiler_params=pltpu.CompilerParams(vmem_limit_bytes=VMEM_LIMIT),
        cost_estimate=pl.CostEstimate(flops=flops, bytes_accessed=moved, transcendentals=0),
        name=name,
    )


def copied(rows, *after):
    return call(
        touch_kernel,
        "copied",
        jax.ShapeDtypeStruct(rows.shape, rows.dtype),
        [anywhere()] * (1 + len(after)),
        anywhere(),
        [pltpu.SemaphoreType.DMA(())],
        flops=1_000_000,
        moved=1_000_000,
    )(rows, *after)


def exchange(chunks):
    return lax.all_to_all(chunks, "seq", 0, 0, tiled=True)


def on_device(queries, key_values, resid, upstream, w_out, gain, global_ids, random_ids):
    core = lax.axis_index("core")
    swap = [(0, 1), (1, 0)]
    glob_ids = global_ids[0]
    rand_ids = random_ids[0].reshape(NBLK * R)

    with jax.named_scope("gather_w"):
        w_full = lax.all_gather(w_out[0], ("z", "core"), axis=0, tiled=True)

    with jax.named_scope("to_heads"):
        packed = jnp.concatenate([queries[0], key_values[0, 0]], axis=0)
        packed = packed.reshape(3, TOK, N_SEQ, PAIR).transpose(2, 0, 1, 3)
        got = exchange(packed).reshape(N_SEQ, 3, QB, BLOCK, PAIR)

    with jax.named_scope("forward"):
        att = call(
            functools.partial(forward_kernel, 8),
            "attention_forward",
            jax.ShapeDtypeStruct((N_SEQ, QB, BLOCK, PAIR), BF16),
            [smem(), smem(), vmem()],
            vmem(),
            flops=1_000_000_000,
            moved=2_000_000,
        )(glob_ids, rand_ids, got)

    with jax.named_scope("to_tokens"):
        att = exchange(att.reshape(N_SEQ, TOK, PAIR))

    with jax.named_scope("project"):
        grad_sum, grad_att = call(
            project_kernel,
            "project",
            (
                jax.ShapeDtypeStruct((TOK, D), BF16),
                jax.ShapeDtypeStruct((N_SEQ, TOK, PAIR), BF16),
            ),
            [vmem(), anywhere(), vmem(), vmem(), vmem()],
            (hbm(), vmem()),
            [
                pltpu.VMEM((D, D), BF16),
                pltpu.VMEM((TOK, D), F32),
                pltpu.VMEM((TOK, D), BF16),
                pltpu.SemaphoreType.DMA((N_SEQ,)),
                pltpu.SemaphoreType.DMA(()),
            ],
            flops=2_000_000_000,
            moved=10_000_000,
        )(att, w_full, resid[0, 0], upstream[0, 0], gain)

    with jax.named_scope("grad_to_heads"):
        grad_got = exchange(grad_att).reshape(N_SEQ, QB, BLOCK, PAIR)

    with jax.named_scope("weight_grad"):
        other = lax.ppermute(att, "core", swap)
        other_sum = lax.ppermute(grad_sum, "core", swap)
        term = call(
            term_kernel,
            "weight_term",
            jax.ShapeDtypeStruct((N_Z, N_SEQ, HDIM, PAIR), BF16),
            [smem()] + [vmem()] * 4,
            anywhere(),
            [
                pltpu.VMEM((N_Z, N_SEQ, HDIM, PAIR), BF16),
                pltpu.VMEM((2 * TOK, D), BF16),
                pltpu.SemaphoreType.DMA((N_Z,)),
            ],
            flops=1_000_000_000,
            moved=6_000_000,
        )(core.reshape(1).astype(jnp.int32), att, other, grad_sum, other_sum)
        shard = lax.psum_scatter(term, "z", scatter_dimension=0, tiled=True)[0]

    with jax.named_scope("passed"):
        passed = lax.ppermute(copied(grad_sum, grad_got), "section", swap)

    with jax.named_scope("backward"):
        grads = call(
            functools.partial(backward_kernel, 8),
            "attention_backward",
            jax.ShapeDtypeStruct((N_SEQ, 3, QB, BLOCK, PAIR), BF16),
            [smem(), smem(), vmem(), vmem()],
            vmem(),
            [
                pltpu.VMEM((2, NBLK, BLOCK, PAIR), F32),
                pltpu.VMEM((2, NG * BLOCK, PAIR), F32),
                pltpu.VMEM((2, NBLK, BLOCK, PAIR), F32),
            ],
            flops=3_000_000_000,
            moved=4_000_000,
        )(glob_ids, rand_ids, got, grad_got)

    with jax.named_scope("grads_to_tokens"):
        back = exchange(grads.reshape(N_SEQ, 3, TOK, PAIR))

    shard, back = lax.optimization_barrier((shard, back))
    with jax.named_scope("unpack"):
        grad_query, grad_pairs = call(
            unpack_kernel,
            "unpack",
            (
                jax.ShapeDtypeStruct((TOK, D), BF16),
                jax.ShapeDtypeStruct((2, TOK, D), BF16),
            ),
            [anywhere()],
            (anywhere(), anywhere()),
            [pltpu.SemaphoreType.DMA((N_SEQ, 2))],
            flops=1_000_000,
            moved=3_000_000,
        )(back)

    with jax.named_scope("weight_grad"):
        spread = call(
            spread_kernel,
            "weight_sum",
            jax.ShapeDtypeStruct((N_SEQ, HDIM, PAIR), BF16),
            [vmem()],
            vmem(),
            flops=1_000_000,
            moved=1_000_000,
        )(exchange(shard))
        spread, passed = lax.optimization_barrier((spread, passed))
        weight_grad = call(
            average_kernel,
            "average",
            jax.ShapeDtypeStruct((HDIM, D), F32),
            [vmem()],
            hbm(),
            [pltpu.VMEM((HDIM, D), F32), pltpu.SemaphoreType.DMA((N_SEQ,))],
            flops=1_000_000,
            moved=1_500_000,
        )(exchange(spread))

    return (
        grad_query[None, None],
        grad_pairs[None, None],
        copied(passed)[None, None],
        weight_grad[None],
    )


def solution(mesh):
    fine = Mesh(mesh.devices.reshape(8, 2, 8, 2), ("z", "core", "seq", "section"))
    dp = ("z", "core")
    tokens = P("section", dp, "seq", None)
    pairs = P("section", dp, None, "seq", None)
    rows = P("section", dp, None)
    return jax.shard_map(
        on_device,
        mesh=fine,
        in_specs=(
            tokens,
            pairs,
            tokens,
            tokens,
            rows,
            P("section", None),
            P(dp, None),
            P(dp, None, None),
        ),
        out_specs=(tokens, pairs, tokens, rows),
        check_vma=False,
    )
```

```python
import functools
import math

import jax
import jax.numpy as jnp
from jax import lax
from jax.experimental import pallas as pl
from jax.experimental.pallas import tpu as pltpu
from jax.sharding import Mesh
from jax.sharding import PartitionSpec as P

HDIM = 128
BLOCK = 64
R = 3
NG = 2
QB = 2
N_SEQ = 8
NBLK = N_SEQ * QB
PAIR = 2 * HDIM
D = 2048
STAGE = 2
N_Z = 8
BATCH = 16
TOK = QB * BLOCK
LISTED = 3 + NG + R
SCALE = 1.0 / math.sqrt(HDIM)
NEG = -1e30
F32 = jnp.float32
BF16 = jnp.bfloat16
VMEM_LIMIT = 48 * 1024 * 1024


def dot(a, b, contract):
    return lax.dot_general(a, b, (contract, ((), ())), preferred_element_type=F32)


def diagonal(rows):
    zero = jnp.zeros((BLOCK, HDIM), rows.dtype)
    top = jnp.concatenate([rows[:, :HDIM], zero], axis=1)
    low = jnp.concatenate([zero, rows[:, HDIM:]], axis=1)
    return jnp.concatenate([top, low], axis=0)


def undiagonal(both):
    return jnp.concatenate([both[:BLOCK, :HDIM], both[BLOCK:, HDIM:]], axis=1)


def listed_blocks(j, glob_ref, rand_ref):
    window = [jnp.maximum(j - 1, 0), j, jnp.minimum(j + 1, NBLK - 1)]
    chosen = [glob_ref[g] for g in range(NG)]
    chosen += [rand_ref[j * R + r] for r in range(R)]
    return window + chosen


def take(got_ref, which, ids):
    return jnp.concatenate([got_ref[b // QB, which, b % QB] for b in ids], axis=0)


def share_columns(j, keys, query_diag):
    scores = dot(keys, query_diag, ((1,), (1,))) * SCALE
    first = jnp.where(j > 0, scores[:BLOCK], NEG)
    last = jnp.where(j < NBLK - 1, scores[2 * BLOCK : 3 * BLOCK], NEG)
    scores = jnp.concatenate(
        [first, scores[BLOCK : 2 * BLOCK], last, scores[3 * BLOCK :]], axis=0
    )
    top = jnp.max(scores, axis=0, keepdims=True)
    raised = jnp.exp(scores - top)
    total = jnp.sum(raised, axis=0, keepdims=True)
    return raised * (1.0 / total)


def forward_kernel(unroll, glob_ref, rand_ref, got_ref, att_ref):
    def one(j):
        ids = listed_blocks(j, glob_ref, rand_ref)
        keys = take(got_ref, 1, ids)
        values = take(got_ref, 2, ids)
        query_diag = diagonal(got_ref[j // QB, 0, j % QB])
        shares = share_columns(j, keys, query_diag).astype(BF16)
        att = dot(shares, values, ((0,), (0,)))
        att_ref[j // QB, j % QB] = undiagonal(att).astype(BF16)

    def step(g, carry):
        for u in range(unroll):
            one(g * unroll + u)
        return carry

    lax.fori_loop(0, NBLK // unroll, step, 0)


def backward_kernel(unroll, glob_ref, rand_ref, got_ref, grad_ref, out_ref, acc, glob_acc, rand_acc):
    acc[...] = jnp.zeros_like(acc)
    glob_acc[...] = jnp.zeros_like(glob_acc)
    rand_acc[...] = jnp.zeros_like(rand_acc)

    def one(j):
        ids = listed_blocks(j, glob_ref, rand_ref)
        keys = take(got_ref, 1, ids)
        values = take(got_ref, 2, ids)
        query_diag = diagonal(got_ref[j // QB, 0, j % QB])
        grad_diag = diagonal(grad_ref[j // QB, j % QB])
        shares = share_columns(j, keys, query_diag)
        grad_shares = dot(values, grad_diag, ((1,), (1,)))
        centre = jnp.sum(shares * grad_shares, axis=0, keepdims=True)
        grad_scores = (shares * (grad_shares - centre) * SCALE).astype(BF16)
        grad_query = dot(grad_scores, keys, ((0,), (0,)))
        out_ref[j // QB, 0, j % QB] = undiagonal(grad_query).astype(BF16)
        parts = (
            dot(grad_scores, query_diag, ((1,), (0,))),
            dot(shares.astype(BF16), grad_diag, ((1,), (0,))),
        )
        for which in range(2):
            part = parts[which]
            for n in range(3):
                acc[which, ids[n]] += part[n * BLOCK : (n + 1) * BLOCK]
            glob_acc[which] += part[3 * BLOCK : (3 + NG) * BLOCK]
            for n in range(3 + NG, LISTED):
                rand_acc[which, ids[n]] += part[n * BLOCK : (n + 1) * BLOCK]

    def step(g, carry):
        for u in range(unroll):
            one(g * unroll + u)
        return carry

    lax.fori_loop(0, NBLK // unroll, step, 0)
    for which in range(2):
        for g in range(NG):
            acc[which, glob_ref[g]] += glob_acc[which, g * BLOCK : (g + 1) * BLOCK]

    def finish(b, carry):
        for which in range(2):
            total = acc[which, b] + rand_acc[which, b]
            out_ref[b // QB, 1 + which, b % QB] = total.astype(BF16)
        return carry

    lax.fori_loop(0, NBLK, finish, 0)


def weight_copies(w_hbm, w_vmem, sems):
    copies = []
    for n in range(N_SEQ // STAGE):
        rows = pl.ds(n * STAGE * PAIR, STAGE * PAIR)
        copies.append(pltpu.make_async_copy(w_hbm.at[rows], w_vmem.at[rows], sems.at[n]))
    for copy in copies:
        copy.start()
    return copies


def project_kernel(att_ref, w_hbm, resid_ref, up_ref, gain_ref, sum_ref, w_vmem, total, sems):
    copies = weight_copies(w_hbm, w_vmem, sems)
    for n in range(N_SEQ // STAGE):
        copies[n].wait()
        att = jnp.concatenate([att_ref[s] for s in range(n * STAGE, (n + 1) * STAGE)], axis=1)
        part = dot(att, w_vmem[n * STAGE * PAIR : (n + 1) * STAGE * PAIR], ((1,), (0,)))
        total[...] = part + (resid_ref[...].astype(F32) if n == 0 else total[...])
    summed = total[...]
    inverse = lax.rsqrt(jnp.mean(summed * summed, axis=-1, keepdims=True) + 1e-06)
    scaled = up_ref[...].astype(F32) * gain_ref[...]
    inner = jnp.mean(scaled * summed, axis=-1, keepdims=True)
    grad_sum = inverse * scaled - summed * (inverse * inverse * inverse * inner)
    sum_ref[...] = grad_sum.astype(BF16)


def grad_kernel(sum_ref, w_hbm, ga_ref, w_vmem, sems):
    copies = weight_copies(w_hbm, w_vmem, sems)
    for n in range(N_SEQ // STAGE):
        copies[n].wait()
        for s in range(n * STAGE, (n + 1) * STAGE):
            part = dot(sum_ref[...], w_vmem[s * PAIR : (s + 1) * PAIR], ((1,), (1,)))
            ga_ref[s] = part.astype(BF16)


def term_kernel(core_ref, own_ref, other_ref, own_sum_ref, other_sum_ref, out_hbm, held, sums, sems):
    columns = pl.ds(pl.multiple_of(core_ref[0] * HDIM, HDIM), HDIM)
    sums[:TOK] = own_sum_ref[...]
    sums[TOK:] = other_sum_ref[...]
    copies = []
    for n in range(N_Z):
        both = jnp.concatenate([own_ref[n, :, columns], other_ref[n, :, columns]], axis=0)
        part = dot(both, sums[...], ((0,), (0,))).astype(BF16)
        for s in range(N_SEQ):
            held[n, s] = part[:, s * PAIR : (s + 1) * PAIR]
        copies.append(pltpu.make_async_copy(held.at[n], out_hbm.at[n], sems.at[n]))
        copies[-1].start()
    for copy in copies:
        copy.wait()


def touch_kernel(rows_hbm, *refs):
    out_hbm, sem = refs[-2:]
    copy = pltpu.make_async_copy(rows_hbm, out_hbm, sem)
    copy.start()
    copy.wait()


def unpack_kernel(back_hbm, query_hbm, pairs_hbm, sems):
    copies = []
    for s in range(N_SEQ):
        at = pl.ds(s * PAIR, PAIR)
        copies += [
            pltpu.make_async_copy(back_hbm.at[s, 0], query_hbm.at[:, at], sems.at[s, 0]),
            pltpu.make_async_copy(
                back_hbm.at[s, pl.ds(1, 2)], pairs_hbm.at[:, :, at], sems.at[s, 1]
            ),
        ]
    for copy in copies:
        copy.start()
    for copy in copies:
        copy.wait()


def spread_kernel(parts_ref, out_ref):
    total = parts_ref[0].astype(F32)
    for n in range(1, N_SEQ):
        total += parts_ref[n].astype(F32)
    total = total.astype(BF16)
    for s in range(N_SEQ):
        out_ref[s] = total


def average_kernel(pieces_ref, out_hbm, held, sems):
    copies = []
    for s in range(N_SEQ):
        at = pl.ds(s * PAIR, PAIR)
        held[:, at] = pieces_ref[s].astype(F32) * (1.0 / BATCH)
        copies.append(pltpu.make_async_copy(held.at[:, at], out_hbm.at[:, at], sems.at[s]))
        copies[-1].start()
    for copy in copies:
        copy.wait()


def vmem():
    return pl.BlockSpec(memory_space=pltpu.VMEM)


def hbm():
    return pl.BlockSpec(memory_space=pltpu.HBM)


def anywhere():
    return pl.BlockSpec(memory_space=pl.ANY)


def smem():
    return pl.BlockSpec(memory_space=pltpu.SMEM)


def call(kernel, name, out_shape, in_specs, out_specs, scratch=(), flops=0, moved=0):
    return pl.pallas_call(
        kernel,
        out_shape=out_shape,
        in_specs=in_specs,
        out_specs=out_specs,
        scratch_shapes=list(scratch),
        compiler_params=pltpu.CompilerParams(vmem_limit_bytes=VMEM_LIMIT),
        cost_estimate=pl.CostEstimate(flops=flops, bytes_accessed=moved, transcendentals=0),
        name=name,
    )


def copied(rows, *after):
    return call(
        touch_kernel,
        "copied",
        jax.ShapeDtypeStruct(rows.shape, rows.dtype),
        [anywhere()] * (1 + len(after)),
        anywhere(),
        [pltpu.SemaphoreType.DMA(())],
        flops=1_000_000,
        moved=1_000_000,
    )(rows, *after)


def exchange(chunks):
    return lax.all_to_all(chunks, "seq", 0, 0, tiled=True)


def on_device(queries, key_values, resid, upstream, w_out, gain, global_ids, random_ids):
    core = lax.axis_index("core")
    swap = [(0, 1), (1, 0)]
    glob_ids = global_ids[0]
    rand_ids = random_ids[0].reshape(NBLK * R)

    with jax.named_scope("gather_w"):
        w_full = lax.all_gather(w_out[0], ("z", "core"), axis=0, tiled=True)

    with jax.named_scope("to_heads"):
        packed = jnp.concatenate([queries[0], key_values[0, 0]], axis=0)
        packed = packed.reshape(3, TOK, N_SEQ, PAIR).transpose(2, 0, 1, 3)
        got = exchange(packed).reshape(N_SEQ, 3, QB, BLOCK, PAIR)

    with jax.named_scope("forward"):
        att = call(
            functools.partial(forward_kernel, 8),
            "attention_forward",
            jax.ShapeDtypeStruct((N_SEQ, QB, BLOCK, PAIR), BF16),
            [smem(), smem(), vmem()],
            vmem(),
            flops=1_000_000_000,
            moved=2_000_000,
        )(glob_ids, rand_ids, got)

    with jax.named_scope("to_tokens"):
        att = exchange(att.reshape(N_SEQ, TOK, PAIR))

    with jax.named_scope("project"):
        scratch = [pltpu.VMEM((D, D), BF16), pltpu.SemaphoreType.DMA((N_SEQ // STAGE,))]
        grad_sum = call(
            project_kernel,
            "project",
            jax.ShapeDtypeStruct((TOK, D), BF16),
            [vmem(), anywhere(), vmem(), vmem(), vmem()],
            vmem(),
            [scratch[0], pltpu.VMEM((TOK, D), F32), scratch[1]],
            flops=1_000_000_000,
            moved=9_000_000,
        )(att, w_full, resid[0, 0], upstream[0, 0], gain)
        grad_att = call(
            grad_kernel,
            "grad_attended",
            jax.ShapeDtypeStruct((N_SEQ, TOK, PAIR), BF16),
            [vmem(), anywhere()],
            vmem(),
            scratch,
            flops=1_000_000_000,
            moved=9_000_000,
        )(grad_sum, w_full)

    with jax.named_scope("grad_to_heads"):
        grad_got = exchange(grad_att).reshape(N_SEQ, QB, BLOCK, PAIR)

    with jax.named_scope("weight_grad"):
        other = lax.ppermute(att, "core", swap)
        other_sum = lax.ppermute(grad_sum, "core", swap)
        term = call(
            term_kernel,
            "weight_term",
            jax.ShapeDtypeStruct((N_Z, N_SEQ, HDIM, PAIR), BF16),
            [smem()] + [vmem()] * 4,
            anywhere(),
            [
                pltpu.VMEM((N_Z, N_SEQ, HDIM, PAIR), BF16),
                pltpu.VMEM((2 * TOK, D), BF16),
                pltpu.SemaphoreType.DMA((N_Z,)),
            ],
            flops=1_000_000_000,
            moved=6_000_000,
        )(core.reshape(1).astype(jnp.int32), att, other, grad_sum, other_sum)
        shard = lax.psum_scatter(term, "z", scatter_dimension=0, tiled=True)[0]

    with jax.named_scope("passed"):
        passed = lax.ppermute(grad_sum, "section", swap)

    with jax.named_scope("backward"):
        grads = call(
            functools.partial(backward_kernel, 8),
            "attention_backward",
            jax.ShapeDtypeStruct((N_SEQ, 3, QB, BLOCK, PAIR), BF16),
            [smem(), smem(), vmem(), vmem()],
            vmem(),
            [
                pltpu.VMEM((2, NBLK, BLOCK, PAIR), F32),
                pltpu.VMEM((2, NG * BLOCK, PAIR), F32),
                pltpu.VMEM((2, NBLK, BLOCK, PAIR), F32),
            ],
            flops=3_000_000_000,
            moved=4_000_000,
        )(glob_ids, rand_ids, got, grad_got)

    grads, passed = lax.optimization_barrier((grads, passed))
    with jax.named_scope("grads_to_tokens"):
        back = exchange(grads.reshape(N_SEQ, 3, TOK, PAIR))

    shard, back = lax.optimization_barrier((shard, back))
    with jax.named_scope("unpack"):
        grad_query, grad_pairs = call(
            unpack_kernel,
            "unpack",
            (
                jax.ShapeDtypeStruct((TOK, D), BF16),
                jax.ShapeDtypeStruct((2, TOK, D), BF16),
            ),
            [anywhere()],
            (anywhere(), anywhere()),
            [pltpu.SemaphoreType.DMA((N_SEQ, 2))],
            flops=1_000_000,
            moved=3_000_000,
        )(back)

    with jax.named_scope("weight_grad"):
        spread = call(
            spread_kernel,
            "weight_sum",
            jax.ShapeDtypeStruct((N_SEQ, HDIM, PAIR), BF16),
            [vmem()],
            vmem(),
            flops=1_000_000,
            moved=1_000_000,
        )(exchange(shard))
        weight_grad = call(
            average_kernel,
            "average",
            jax.ShapeDtypeStruct((HDIM, D), F32),
            [vmem()],
            hbm(),
            [pltpu.VMEM((HDIM, D), F32), pltpu.SemaphoreType.DMA((N_SEQ,))],
            flops=1_000_000,
            moved=1_500_000,
        )(exchange(spread))

    return (
        grad_query[None, None],
        grad_pairs[None, None],
        copied(passed)[None, None],
        weight_grad[None],
    )


def solution(mesh):
    fine = Mesh(mesh.devices.reshape(8, 2, 8, 2), ("z", "core", "seq", "section"))
    dp = ("z", "core")
    tokens = P("section", dp, "seq", None)
    pairs = P("section", dp, None, "seq", None)
    rows = P("section", dp, None)
    return jax.shard_map(
        on_device,
        mesh=fine,
        in_specs=(
            tokens,
            pairs,
            tokens,
            tokens,
            rows,
            P("section", None),
            P(dp, None),
            P(dp, None, None),
        ),
        out_specs=(tokens, pairs, tokens, rows),
        check_vma=False,
    )
```

```python
import functools
import math

import jax
import jax.numpy as jnp
from jax import lax
from jax.experimental import pallas as pl
from jax.experimental.pallas import tpu as pltpu
from jax.sharding import Mesh
from jax.sharding import PartitionSpec as P

HDIM = 128
BLOCK = 64
R = 3
NG = 2
QB = 2
N_SEQ = 8
NBLK = N_SEQ * QB
PAIR = 2 * HDIM
D = 2048
STAGE = 2
N_Z = 8
BATCH = 16
TOK = QB * BLOCK
LISTED = 3 + NG + R
SCALE = 1.0 / math.sqrt(HDIM)
NEG = -1e30
F32 = jnp.float32
BF16 = jnp.bfloat16
VMEM_LIMIT = 48 * 1024 * 1024


def dot(a, b, contract):
    return lax.dot_general(a, b, (contract, ((), ())), preferred_element_type=F32)


def diagonal(rows):
    zero = jnp.zeros((BLOCK, HDIM), rows.dtype)
    top = jnp.concatenate([rows[:, :HDIM], zero], axis=1)
    low = jnp.concatenate([zero, rows[:, HDIM:]], axis=1)
    return jnp.concatenate([top, low], axis=0)


def undiagonal(both):
    return jnp.concatenate([both[:BLOCK, :HDIM], both[BLOCK:, HDIM:]], axis=1)


def listed_blocks(j, glob_ref, rand_ref):
    window = [jnp.maximum(j - 1, 0), j, jnp.minimum(j + 1, NBLK - 1)]
    chosen = [glob_ref[g] for g in range(NG)]
    chosen += [rand_ref[j * R + r] for r in range(R)]
    return window + chosen


def take(got_ref, which, ids):
    return jnp.concatenate([got_ref[b // QB, which, b % QB] for b in ids], axis=0)


def share_columns(j, keys, query_diag):
    scores = dot(keys, query_diag, ((1,), (1,))) * SCALE
    first = jnp.where(j > 0, scores[:BLOCK], NEG)
    last = jnp.where(j < NBLK - 1, scores[2 * BLOCK : 3 * BLOCK], NEG)
    scores = jnp.concatenate(
        [first, scores[BLOCK : 2 * BLOCK], last, scores[3 * BLOCK :]], axis=0
    )
    top = jnp.max(scores, axis=0, keepdims=True)
    raised = jnp.exp(scores - top)
    total = jnp.sum(raised, axis=0, keepdims=True)
    return raised * (1.0 / total)


def forward_kernel(unroll, glob_ref, rand_ref, got_ref, att_ref):
    def one(j):
        ids = listed_blocks(j, glob_ref, rand_ref)
        keys = take(got_ref, 1, ids)
        values = take(got_ref, 2, ids)
        query_diag = diagonal(got_ref[j // QB, 0, j % QB])
        shares = share_columns(j, keys, query_diag).astype(BF16)
        att = dot(shares, values, ((0,), (0,)))
        att_ref[j // QB, j % QB] = undiagonal(att).astype(BF16)

    def step(g, carry):
        for u in range(unroll):
            one(g * unroll + u)
        return carry

    lax.fori_loop(0, NBLK // unroll, step, 0)


def backward_kernel(unroll, glob_ref, rand_ref, got_ref, grad_ref, out_ref, acc, glob_acc, rand_acc):
    acc[...] = jnp.zeros_like(acc)
    glob_acc[...] = jnp.zeros_like(glob_acc)
    rand_acc[...] = jnp.zeros_like(rand_acc)

    def one(j):
        ids = listed_blocks(j, glob_ref, rand_ref)
        keys = take(got_ref, 1, ids)
        values = take(got_ref, 2, ids)
        query_diag = diagonal(got_ref[j // QB, 0, j % QB])
        grad_diag = diagonal(grad_ref[j // QB, j % QB])
        shares = share_columns(j, keys, query_diag)
        grad_shares = dot(values, grad_diag, ((1,), (1,)))
        centre = jnp.sum(shares * grad_shares, axis=0, keepdims=True)
        grad_scores = (shares * (grad_shares - centre) * SCALE).astype(BF16)
        grad_query = dot(grad_scores, keys, ((0,), (0,)))
        out_ref[j // QB, 0, j % QB] = undiagonal(grad_query).astype(BF16)
        parts = (
            dot(grad_scores, query_diag, ((1,), (0,))),
            dot(shares.astype(BF16), grad_diag, ((1,), (0,))),
        )
        for which in range(2):
            part = parts[which]
            for n in range(3):
                acc[which, ids[n]] += part[n * BLOCK : (n + 1) * BLOCK]
            glob_acc[which] += part[3 * BLOCK : (3 + NG) * BLOCK]
            for n in range(3 + NG, LISTED):
                rand_acc[which, ids[n]] += part[n * BLOCK : (n + 1) * BLOCK]

    def step(g, carry):
        for u in range(unroll):
            one(g * unroll + u)
        return carry

    lax.fori_loop(0, NBLK // unroll, step, 0)
    for which in range(2):
        for g in range(NG):
            acc[which, glob_ref[g]] += glob_acc[which, g * BLOCK : (g + 1) * BLOCK]

    def finish(b, carry):
        for which in range(2):
            total = acc[which, b] + rand_acc[which, b]
            out_ref[b // QB, 1 + which, b % QB] = total.astype(BF16)
        return carry

    lax.fori_loop(0, NBLK, finish, 0)


def weight_copies(w_hbm, w_vmem, sems):
    copies = []
    for n in range(N_SEQ // STAGE):
        rows = pl.ds(n * STAGE * PAIR, STAGE * PAIR)
        copies.append(pltpu.make_async_copy(w_hbm.at[rows], w_vmem.at[rows], sems.at[n]))
    for copy in copies:
        copy.start()
    return copies


def project_kernel(att_ref, w_hbm, resid_ref, up_ref, gain_ref, sum_ref, w_vmem, total, sems):
    copies = weight_copies(w_hbm, w_vmem, sems)
    for n in range(N_SEQ // STAGE):
        copies[n].wait()
        att = jnp.concatenate([att_ref[s] for s in range(n * STAGE, (n + 1) * STAGE)], axis=1)
        part = dot(att, w_vmem[n * STAGE * PAIR : (n + 1) * STAGE * PAIR], ((1,), (0,)))
        total[...] = part + (resid_ref[...].astype(F32) if n == 0 else total[...])
    summed = total[...]
    inverse = lax.rsqrt(jnp.mean(summed * summed, axis=-1, keepdims=True) + 1e-06)
    scaled = up_ref[...].astype(F32) * gain_ref[...]
    inner = jnp.mean(scaled * summed, axis=-1, keepdims=True)
    grad_sum = inverse * scaled - summed * (inverse * inverse * inverse * inner)
    sum_ref[...] = grad_sum.astype(BF16)


def grad_kernel(sum_ref, w_hbm, ga_ref, w_vmem, sems):
    copies = weight_copies(w_hbm, w_vmem, sems)
    for n in range(N_SEQ // STAGE):
        copies[n].wait()
        for s in range(n * STAGE, (n + 1) * STAGE):
            part = dot(sum_ref[...], w_vmem[s * PAIR : (s + 1) * PAIR], ((1,), (1,)))
            ga_ref[s] = part.astype(BF16)


def term_kernel(core_ref, own_ref, other_ref, own_sum_ref, other_sum_ref, after, out_hbm, held, sums, sems):
    columns = pl.ds(pl.multiple_of(core_ref[0] * HDIM, HDIM), HDIM)
    sums[:TOK] = own_sum_ref[...]
    sums[TOK:] = other_sum_ref[...]
    copies = []
    for n in range(N_Z):
        both = jnp.concatenate([own_ref[n, :, columns], other_ref[n, :, columns]], axis=0)
        part = dot(both, sums[...], ((0,), (0,))).astype(BF16)
        for s in range(N_SEQ):
            held[n, s] = part[:, s * PAIR : (s + 1) * PAIR]
        copies.append(pltpu.make_async_copy(held.at[n], out_hbm.at[n], sems.at[n]))
        copies[-1].start()
    for copy in copies:
        copy.wait()


def touch_kernel(rows_hbm, *refs):
    out_hbm, sem = refs[-2:]
    copy = pltpu.make_async_copy(rows_hbm, out_hbm, sem)
    copy.start()
    copy.wait()


def unpack_kernel(back_hbm, query_hbm, pairs_hbm, sems):
    copies = []
    for s in range(N_SEQ):
        at = pl.ds(s * PAIR, PAIR)
        copies += [
            pltpu.make_async_copy(back_hbm.at[s, 0], query_hbm.at[:, at], sems.at[s, 0]),
            pltpu.make_async_copy(
                back_hbm.at[s, pl.ds(1, 2)], pairs_hbm.at[:, :, at], sems.at[s, 1]
            ),
        ]
    for copy in copies:
        copy.start()
    for copy in copies:
        copy.wait()


def spread_kernel(parts_ref, out_ref):
    total = parts_ref[0].astype(F32)
    for n in range(1, N_SEQ):
        total += parts_ref[n].astype(F32)
    total = total.astype(BF16)
    for s in range(N_SEQ):
        out_ref[s] = total


def average_kernel(pieces_ref, out_hbm, held, sems):
    copies = []
    for s in range(N_SEQ):
        at = pl.ds(s * PAIR, PAIR)
        held[:, at] = pieces_ref[s].astype(F32) * (1.0 / BATCH)
        copies.append(pltpu.make_async_copy(held.at[:, at], out_hbm.at[:, at], sems.at[s]))
        copies[-1].start()
    for copy in copies:
        copy.wait()


def vmem():
    return pl.BlockSpec(memory_space=pltpu.VMEM)


def hbm():
    return pl.BlockSpec(memory_space=pltpu.HBM)


def anywhere():
    return pl.BlockSpec(memory_space=pl.ANY)


def smem():
    return pl.BlockSpec(memory_space=pltpu.SMEM)


def call(kernel, name, out_shape, in_specs, out_specs, scratch=(), flops=0, moved=0):
    return pl.pallas_call(
        kernel,
        out_shape=out_shape,
        in_specs=in_specs,
        out_specs=out_specs,
        scratch_shapes=list(scratch),
        compiler_params=pltpu.CompilerParams(vmem_limit_bytes=VMEM_LIMIT),
        cost_estimate=pl.CostEstimate(flops=flops, bytes_accessed=moved, transcendentals=0),
        name=name,
    )


def copied(rows, *after):
    return call(
        touch_kernel,
        "copied",
        jax.ShapeDtypeStruct(rows.shape, rows.dtype),
        [anywhere()] * (1 + len(after)),
        anywhere(),
        [pltpu.SemaphoreType.DMA(())],
        flops=1_000_000,
        moved=1_000_000,
    )(rows, *after)


def exchange(chunks):
    return lax.all_to_all(chunks, "seq", 0, 0, tiled=True)


def on_device(queries, key_values, resid, upstream, w_out, gain, global_ids, random_ids):
    core = lax.axis_index("core")
    swap = [(0, 1), (1, 0)]
    glob_ids = global_ids[0]
    rand_ids = random_ids[0].reshape(NBLK * R)

    with jax.named_scope("gather_w"):
        w_full = lax.all_gather(w_out[0], ("z", "core"), axis=0, tiled=True)

    with jax.named_scope("to_heads"):
        packed = jnp.concatenate([queries[0], key_values[0, 0]], axis=0)
        packed = packed.reshape(3, TOK, N_SEQ, PAIR).transpose(2, 0, 1, 3)
        got = exchange(packed).reshape(N_SEQ, 3, QB, BLOCK, PAIR)

    with jax.named_scope("forward"):
        att = call(
            functools.partial(forward_kernel, 8),
            "attention_forward",
            jax.ShapeDtypeStruct((N_SEQ, QB, BLOCK, PAIR), BF16),
            [smem(), smem(), vmem()],
            vmem(),
            flops=1_000_000_000,
            moved=2_000_000,
        )(glob_ids, rand_ids, got)

    with jax.named_scope("to_tokens"):
        att = exchange(att.reshape(N_SEQ, TOK, PAIR))

    with jax.named_scope("project"):
        scratch = [pltpu.VMEM((D, D), BF16), pltpu.SemaphoreType.DMA((N_SEQ // STAGE,))]
        grad_sum = call(
            project_kernel,
            "project",
            jax.ShapeDtypeStruct((TOK, D), BF16),
            [vmem(), anywhere(), vmem(), vmem(), vmem()],
            vmem(),
            [scratch[0], pltpu.VMEM((TOK, D), F32), scratch[1]],
            flops=1_000_000_000,
            moved=9_000_000,
        )(att, w_full, resid[0, 0], upstream[0, 0], gain)
        grad_att = call(
            grad_kernel,
            "grad_attended",
            jax.ShapeDtypeStruct((N_SEQ, TOK, PAIR), BF16),
            [vmem(), anywhere()],
            vmem(),
            scratch,
            flops=1_000_000_000,
            moved=9_000_000,
        )(grad_sum, w_full)

    with jax.named_scope("grad_to_heads"):
        grad_got = exchange(grad_att).reshape(N_SEQ, QB, BLOCK, PAIR)

    with jax.named_scope("weight_grad"):
        other = lax.ppermute(att, "core", swap)
        other_sum = lax.ppermute(grad_sum, "core", swap)
        term = call(
            term_kernel,
            "weight_term",
            jax.ShapeDtypeStruct((N_Z, N_SEQ, HDIM, PAIR), BF16),
            [smem()] + [vmem()] * 4 + [anywhere()],
            anywhere(),
            [
                pltpu.VMEM((N_Z, N_SEQ, HDIM, PAIR), BF16),
                pltpu.VMEM((2 * TOK, D), BF16),
                pltpu.SemaphoreType.DMA((N_Z,)),
            ],
            flops=1_000_000_000,
            moved=6_000_000,
        )(core.reshape(1).astype(jnp.int32), att, other, grad_sum, other_sum, grad_att)
        shard = lax.psum_scatter(term, "z", scatter_dimension=0, tiled=True)[0]

    with jax.named_scope("passed"):
        passed = lax.ppermute(grad_sum, "section", swap)

    with jax.named_scope("backward"):
        grads = call(
            functools.partial(backward_kernel, 8),
            "attention_backward",
            jax.ShapeDtypeStruct((N_SEQ, 3, QB, BLOCK, PAIR), BF16),
            [smem(), smem(), vmem(), vmem()],
            vmem(),
            [
                pltpu.VMEM((2, NBLK, BLOCK, PAIR), F32),
                pltpu.VMEM((2, NG * BLOCK, PAIR), F32),
                pltpu.VMEM((2, NBLK, BLOCK, PAIR), F32),
            ],
            flops=3_000_000_000,
            moved=4_000_000,
        )(glob_ids, rand_ids, got, grad_got)

    grads, passed = lax.optimization_barrier((grads, passed))
    with jax.named_scope("grads_to_tokens"):
        back = exchange(grads.reshape(N_SEQ, 3, TOK, PAIR))

    shard, back = lax.optimization_barrier((shard, back))
    with jax.named_scope("unpack"):
        grad_query, grad_pairs = call(
            unpack_kernel,
            "unpack",
            (
                jax.ShapeDtypeStruct((TOK, D), BF16),
                jax.ShapeDtypeStruct((2, TOK, D), BF16),
            ),
            [anywhere()],
            (anywhere(), anywhere()),
            [pltpu.SemaphoreType.DMA((N_SEQ, 2))],
            flops=1_000_000,
            moved=3_000_000,
        )(back)

    with jax.named_scope("weight_grad"):
        spread = call(
            spread_kernel,
            "weight_sum",
            jax.ShapeDtypeStruct((N_SEQ, HDIM, PAIR), BF16),
            [vmem()],
            vmem(),
            flops=1_000_000,
            moved=1_000_000,
        )(exchange(shard))
        weight_grad = call(
            average_kernel,
            "average",
            jax.ShapeDtypeStruct((HDIM, D), F32),
            [vmem()],
            hbm(),
            [pltpu.VMEM((HDIM, D), F32), pltpu.SemaphoreType.DMA((N_SEQ,))],
            flops=1_000_000,
            moved=1_500_000,
        )(exchange(spread))

    return (
        grad_query[None, None],
        grad_pairs[None, None],
        copied(passed)[None, None],
        weight_grad[None],
    )


def solution(mesh):
    fine = Mesh(mesh.devices.reshape(8, 2, 8, 2), ("z", "core", "seq", "section"))
    dp = ("z", "core")
    tokens = P("section", dp, "seq", None)
    pairs = P("section", dp, None, "seq", None)
    rows = P("section", dp, None)
    return jax.shard_map(
        on_device,
        mesh=fine,
        in_specs=(
            tokens,
            pairs,
            tokens,
            tokens,
            rows,
            P("section", None),
            P(dp, None),
            P(dp, None, None),
        ),
        out_specs=(tokens, pairs, tokens, rows),
        check_vma=False,
    )
```
